32 devices in a mesh: groups: 2 (over y), angle: 4 (over z), slab: 2 (over x), row: 2 (over core).
Axes of the slice: x: 2, y: 2, z: 4, core: 2. Of those that a mesh axis runs over, the one named last changes fastest.
Arguments:
- projections: bfloat16 [32, 256, 2048], P(('groups', 'angle'), ('slab', 'row')), parts along dimension 0, may hold values from -24 to 24
- tile_lists: int32 [32, 4, 2], P(('groups', 'angle'), ('slab', 'row')), parts along dimension 0, may hold values from 0 to 3, as said below
- band_weights: bfloat16 [32, 8, 32, 4], P(('groups', 'angle'), None, ('slab', 'row')), parts along dimension 0, may hold values from 0.099609375 to 1
- band_offsets: int32 [32, 8, 32], P(('groups', 'angle'), None, ('slab', 'row')), parts along dimension 0, may hold values from 0 to 124
Outputs:
- volume: float32 [16, 32, 2048], P(('groups', 'angle'), ('slab', 'row')), parts along dimension 0
The draws below stay inside these ranges and needn't reach their ends.
There are 2 independent parts, one for each index of `groups`. The reference program is written for one: setup_inputs(seed, part) draws one part's arguments, and reference() takes and returns one part's arrays. A program takes and returns all parts, laid end to end along the dimension named above; each array names one. Nothing has to cross between parts.
Inputs may be any that keep to these rules, and one draw needn't show every extreme that they name: `tile_lists`: each list holds 2 consecutive tile numbers in increasing order, starting at 0 or at 2; within the 4 views of one angle sector, one slab group lists one tile in at most 2 views, and some group reaches that.
All inputs are finite; a program needn't handle non-finite values.
Results may differ from the reference program's by a relative error of at most 0.0035.
Values may be sent and summed in bfloat16 or wider, within the bound.
A program may use at most 64 MiB of HBM per device.

```python
import math
import jax
import jax.numpy as jnp
from jax import lax

COLS = 2048
TILE_ROWS = 64
NEED = 2
BAND = 4
VIEW_DEV = 4
Z_GROUP = 8
TILES = 4
ROWS = 256
VIEWS = 16
Z_ALL = 32
Y_ALL = 8


def draw_tile_lists(key, part):
    key = jax.random.fold_in(key, 11)
    sectors = VIEWS // VIEW_DEV
    scores = jax.random.randint(key, (sectors, TILES, VIEW_DEV), 0, 1048576) * VIEW_DEV
    scores = scores + jnp.arange(VIEW_DEV, dtype=jnp.int32)[None, None, :]
    ranks = jnp.argsort(jnp.argsort(scores, axis=-1), axis=-1).astype(jnp.int32)
    parity = (jnp.arange(TILES, dtype=jnp.int32) % 2)[None, :, None]
    lower = ranks * 2 + parity < VIEW_DEV
    starts = jnp.where(lower, 0, TILES - NEED).astype(jnp.int32)
    starts = jnp.transpose(starts, (0, 2, 1)).reshape(VIEWS, TILES)
    return (starts[:, :, None] + jnp.arange(NEED, dtype=jnp.int32)[None, None, :]).astype(jnp.int32)


def place_ends(result, stream_key, least, top_value):
    index_at = [jax.random.randint(jax.random.fold_in(stream_key, axis), (), 0, length) for axis, length in enumerate(result.shape)]
    longest = result.shape.index(max(result.shape))
    next_to = index_at[:longest] + [(index_at[longest] + 1) % result.shape[longest]] + index_at[longest + 1:]
    return result.at[tuple(index_at)].set(least).at[tuple(next_to)].set(top_value)


def block_levels(stream_key, extent, cuts, least, high):
    def one(axis_at, blocks):
        heights = jax.random.uniform(jax.random.fold_in(jax.random.fold_in(stream_key, 6), axis_at), (blocks,), jnp.float32, least / len(cuts), high / len(cuts))
        return jnp.repeat(jnp.exp(heights), extent[axis_at] // blocks).reshape((-1,) + (1,) * (len(extent) - axis_at - 1))

    loudness = one(*cuts[0])
    for cut in cuts[1:]:
        loudness = loudness * one(*cut)
    return loudness


def noise(stream_key, extent, width, bound, split=(), held_as=jnp.bfloat16):
    entries = jax.random.normal(stream_key, extent, jnp.float32) * width
    if len(split) > 0:
        entries = block_levels(stream_key, extent, split, -0.22, 0.18) * entries
    return jnp.clip(entries, min=-bound, max=bound).astype(held_as)


def setup_inputs(seed: int = 0, part: int = 0) -> dict:
    keys = jax.random.split(jax.random.key(seed), 5)
    own_keys = jax.random.split(jax.random.fold_in(keys[4], part), 5)
    return {
        "projections": noise(own_keys[0], (VIEWS, ROWS, COLS), 4.0, 24.0, ((0, 4), (1, 4))),
        "tile_lists": draw_tile_lists(jax.random.fold_in(jax.random.fold_in(keys[4], part), 71), part),
        "band_weights": jnp.clip(0.099609375 + 0.9003906 * jax.random.uniform(own_keys[2], (VIEWS, Y_ALL, Z_ALL, BAND), jnp.float32) ** block_levels(own_keys[2], (VIEWS, Y_ALL, Z_ALL, BAND), ((0, 4), (2, 4)), -0.2, 0.2), 0.099609375, 1.0).astype(jnp.bfloat16),
        "band_offsets": place_ends(jax.random.randint(own_keys[3], (VIEWS, Y_ALL, Z_ALL), 0, NEED * TILE_ROWS - BAND + 1), jax.random.fold_in(own_keys[3], 1), 0, NEED * TILE_ROWS - BAND).astype(jnp.int32),
    }


def ramp_block(detector_cols, first_col, block_cols):
    row_pos = lax.broadcasted_iota(jnp.float32, (detector_cols, block_cols), 0)
    col_pos = lax.broadcasted_iota(jnp.float32, (detector_cols, block_cols), 1) + first_col
    distance = col_pos - row_pos
    parity = jnp.abs(distance) % 2.0
    safe_gap = jnp.where(distance == 0.0, 1.0, distance)
    taps = jnp.where(distance == 0.0, 0.25, jnp.where(parity == 1.0, -1.0 / (math.pi * math.pi * safe_gap * safe_gap), 0.0))
    return taps.astype(jnp.bfloat16)


def ramp_filter(projection):
    view_count, row_count, detector_cols = projection.shape
    flattened = projection.reshape(view_count * row_count, detector_cols)
    block_cols = min(detector_cols, 512)
    pieces = [jnp.dot(flattened, ramp_block(detector_cols, first_col, block_cols), preferred_element_type=jnp.float32) for first_col in range(0, detector_cols, block_cols)]
    return jnp.concatenate(pieces, axis=1).astype(jnp.bfloat16).reshape(view_count, row_count, detector_cols)


def reference(projections, tile_lists, band_weights, band_offsets):
    view_count, row_count, detector_cols = projections.shape
    filtered = ramp_filter(projections)
    y_total = band_weights.shape[1]
    z_total = band_weights.shape[2]
    group_of_z = jnp.arange(z_total, dtype=jnp.int32) // Z_GROUP

    def one_view(total, inputs):
        frame, listed, offsets, weights = inputs
        listed_z = listed[group_of_z]
        listed_full = jnp.broadcast_to(listed_z[None, :, :], (y_total, z_total, NEED))
        local_rows = offsets[:, :, None] + jnp.arange(BAND, dtype=jnp.int32)[None, None, :]
        tile_pick = jnp.take_along_axis(listed_full, (local_rows // TILE_ROWS).astype(jnp.int32), axis=2)
        detector_rows = (tile_pick * TILE_ROWS + local_rows % TILE_ROWS).astype(jnp.int32)
        picked_rows = frame[detector_rows].astype(jnp.float32)
        added = jnp.einsum("yzb,yzbu->yzu", weights.astype(jnp.float32), picked_rows)
        return total + added, None

    start_total = jnp.zeros((y_total, z_total, detector_cols), jnp.float32)
    total, _ = lax.scan(one_view, start_total, (filtered, tile_lists, band_offsets, band_weights))
    return total * (math.pi / view_count)
```

```python
import functools
import math

import jax
import jax.numpy as jnp
import ml_dtypes
import numpy as np
from jax import lax
from jax.experimental import pallas as pl
from jax.experimental.pallas import tpu as pltpu
from jax.sharding import PartitionSpec as P

MESH = pl.DeviceIdType.MESH
CHUNK = 256


def ramp_strip(detector_cols, width):
    rows = np.arange(2 * detector_cols - width)[:, None]
    gap = np.arange(width)[None, :] + (detector_cols - width) - rows
    gap32 = np.where(gap == 0, 1, gap).astype(np.float32)
    scale = np.float32(math.pi * math.pi)
    odd = np.where(gap % 2 != 0, np.float32(-1.0) / (scale * gap32 * gap32), np.float32(0.0))
    return np.where(gap == 0, np.float32(0.25), odd).astype(ml_dtypes.bfloat16)


def fused_kernel(
    angles, scale,
    x_hbm, lists_hbm, weights_hbm, offsets_hbm, strip_hbm,
    out_ref,
    x_v, lists_v, weights_v, offsets_v, strip_v,
    dense, wmat, keep, core_out, core_in, slab_out, slab_in, angle_out, angle_in,
    load_sem, wsend_sem, wrecv_sem, csend_sem, crecv_sem, ssend_sem, srecv_sem, asend_sem, arecv_sem,
):
    views, tile_rows, cols = x_v.shape
    ys, zs, band = weights_v.shape[1:]
    lines = ys * zs
    share = lines // angles
    depth = views * tile_rows
    chunks = cols // CHUNK
    angle = lax.axis_index("angle")
    slab = lax.axis_index("slab")
    row = lax.axis_index("row")

    barrier = pltpu.get_barrier_semaphore()
    near = [
        (1 - slab, 1 - row),
        (slab, 1 - row),
        (1 - slab, row),
    ]
    near_ids = [{"slab": s, "row": r} for s, r in near]
    far_ids = [{"angle": lax.rem(angle + j, angles)} for j in range(1, angles)]
    for device in near_ids + far_ids:
        pl.semaphore_signal(barrier, inc=1, device_id=device, device_id_type=MESH)

    loads = [
        pltpu.make_async_copy(src, dst, load_sem.at[i])
        for i, (src, dst) in enumerate(
            [
                (lists_hbm, lists_v),
                (weights_hbm, weights_v),
                (offsets_hbm, offsets_v),
                (x_hbm, x_v),
                (strip_hbm, strip_v),
            ]
        )
    ]
    for load in loads:
        load.start()
    for load in loads[:3]:
        load.wait()

    lane = lax.broadcasted_iota(jnp.int32, (lines, 2 * tile_rows), 1)
    second = lane >= tile_rows
    within = jnp.where(second, lane - tile_rows, lane)
    same = lax.broadcasted_iota(jnp.int32, (zs, zs), 0) == lax.broadcasted_iota(jnp.int32, (zs, zs), 1)
    first_row, taps = [], []
    for v in range(views):
        offs = offsets_v[v].astype(jnp.float32)
        column = jnp.concatenate(
            [
                jnp.sum(jnp.where(same, offs[y : y + 1, :], 0.0), axis=1, keepdims=True)
                for y in range(ys)
            ],
            axis=0,
        )
        start = lists_v[v].astype(jnp.float32)[:, 0:1] * float(tile_rows)
        first_row.append(column + start)
        taps.append(weights_v[v].astype(jnp.float32).reshape(lines, band))
    places = near + [(slab, row)]
    for pair in range(views // 2):
        a, b = 2 * pair, 2 * pair + 1
        pos = jnp.where(second, first_row[b], first_row[a])
        tap = [jnp.where(second, taps[b][:, k : k + 1], taps[a][:, k : k + 1]) for k in range(band)]
        for slot, (s, r) in enumerate(places):
            gap = (within + (s * 2 + r) * tile_rows).astype(jnp.float32) - pos
            total = jnp.zeros((lines, 2 * tile_rows), jnp.float32)
            for k in range(band):
                total = total + jnp.where(gap == float(k), tap[k], 0.0)
            where = pl.ds(pair * 2 * tile_rows, 2 * tile_rows)
            if slot < 3:
                dense[slot, :, where] = total.astype(jnp.bfloat16)
            else:
                wmat[slot, :, where] = total.astype(jnp.bfloat16)

    pl.semaphore_wait(barrier, len(near_ids) + len(far_ids))
    wcopies = [
        pltpu.make_async_remote_copy(
            src_ref=dense.at[slot],
            dst_ref=wmat.at[slot],
            send_sem=wsend_sem.at[slot],
            recv_sem=wrecv_sem.at[slot],
            device_id=near_ids[slot],
            device_id_type=MESH,
        )
        for slot in range(3)
    ]
    for copy in wcopies:
        copy.start()
    for load in loads[3:]:
        load.wait()

    def core_copy(c):
        return pltpu.make_async_remote_copy(
            src_ref=core_out.at[c], dst_ref=core_in.at[c],
            send_sem=csend_sem.at[c], recv_sem=crecv_sem.at[c],
            device_id=near_ids[1], device_id_type=MESH,
        )

    def slab_copy(c):
        return pltpu.make_async_remote_copy(
            src_ref=slab_out.at[c], dst_ref=slab_in.at[c],
            send_sem=ssend_sem.at[c], recv_sem=srecv_sem.at[c],
            device_id=near_ids[2], device_id_type=MESH,
        )

    def angle_copy(c, j):
        there = pl.multiple_of(lax.rem(angle + j, angles) * share, share)
        return pltpu.make_async_remote_copy(
            src_ref=angle_out.at[c, pl.ds(there, share)], dst_ref=angle_in.at[c, j - 1],
            send_sem=asend_sem.at[c, j - 1], recv_sem=arecv_sem.at[c, j - 1],
            device_id=far_ids[j - 1], device_id_type=MESH,
        )

    def filter_chunk(c):
        rows = pl.ds((chunks - 1 - c) * CHUNK, cols)
        return jnp.dot(
            x_v[...].reshape(depth, cols), strip_v[rows, :], preferred_element_type=jnp.float32
        ).astype(jnp.bfloat16)

    def project_chunk(c, filtered):
        part = jnp.dot(
            wmat[...].reshape(4 * lines, depth), filtered, preferred_element_type=jnp.float32
        )
        core_out[c] = part[: 2 * lines].astype(jnp.bfloat16)
        core_copy(c).start()
        keep[c] = part[2 * lines :]

    def core_step(c):
        core_copy(c).wait_recv()
        slab_out[c] = (keep[c, :lines] + core_in[c, :lines].astype(jnp.float32)).astype(jnp.bfloat16)
        slab_copy(c).start()
        keep[c, lines:] = keep[c, lines:] + core_in[c, lines:].astype(jnp.float32)

    def slab_step(c):
        slab_copy(c).wait_recv()
        total = keep[c, lines:] + slab_in[c].astype(jnp.float32)
        angle_out[c] = total.astype(jnp.bfloat16)
        for j in range(1, angles):
            angle_copy(c, j).start()
        keep[c, lines:] = total

    def angle_step(c):
        here = pl.multiple_of(angle * share, share)
        total = keep[c, pl.ds(lines + here, share)]
        for j in range(1, angles):
            angle_copy(c, j).wait_recv()
            total = total + angle_in[c, j - 1].astype(jnp.float32)
        out_ref[:, :, c * CHUNK : (c + 1) * CHUNK] = (total * scale).reshape(
            share // zs, zs, CHUNK
        )

    lead = 1
    filtered = {}
    for step in range(chunks + lead + 7):
        if step < chunks:
            filtered[step] = filter_chunk(step)
        c = step - lead
        if c == 0:
            for copy in wcopies:
                copy.wait_recv()
        if 0 <= c < chunks:
            project_chunk(c, filtered.pop(c))
        for late, act in ((2, core_step), (4, slab_step), (7, angle_step)):
            if 0 <= c - late + 0 < chunks:
                act(c - late)
    for copy in wcopies:
        copy.wait_send()
    for c in range(chunks):
        core_copy(c).wait_send()
        slab_copy(c).wait_send()
        for j in range(1, angles):
            angle_copy(c, j).wait_send()


def fused_body(angles, projections, tile_lists, band_weights, band_offsets):
    views, tile_rows, cols = projections.shape
    ys, zs, band = band_weights.shape[1:]
    lines = ys * zs
    share = lines // angles
    chunks = cols // CHUNK
    strip = jnp.asarray(ramp_strip(cols, CHUNK))
    bf16, f32 = jnp.bfloat16, jnp.float32
    dma = pltpu.SemaphoreType.DMA
    return pl.pallas_call(
        functools.partial(fused_kernel, angles, math.pi / (views * angles)),
        out_shape=jax.ShapeDtypeStruct((ys // angles, zs, cols), f32),
        in_specs=[pl.BlockSpec(memory_space=pl.ANY)] * 5,
        out_specs=pl.BlockSpec(memory_space=pltpu.VMEM),
        scratch_shapes=[
            pltpu.VMEM(projections.shape, bf16),
            pltpu.VMEM(tile_lists.shape, jnp.int32),
            pltpu.VMEM(band_weights.shape, bf16),
            pltpu.VMEM(band_offsets.shape, jnp.int32),
            pltpu.VMEM(strip.shape, bf16),
            pltpu.VMEM((3, lines, views * tile_rows), bf16),
            pltpu.VMEM((4, lines, views * tile_rows), bf16),
            pltpu.VMEM((chunks, 2 * lines, CHUNK), f32),
            pltpu.VMEM((chunks, 2 * lines, CHUNK), bf16),
            pltpu.VMEM((chunks, 2 * lines, CHUNK), bf16),
            pltpu.VMEM((chunks, lines, CHUNK), bf16),
            pltpu.VMEM((chunks, lines, CHUNK), bf16),
            pltpu.VMEM((chunks, lines, CHUNK), bf16),
            pltpu.VMEM((chunks, angles - 1, share, CHUNK), bf16),
            dma((5,)),
            dma((3,)),
            dma((3,)),
            dma((chunks,)),
            dma((chunks,)),
            dma((chunks,)),
            dma((chunks,)),
            dma((chunks, angles - 1)),
            dma((chunks, angles - 1)),
        ],
        compiler_params=pltpu.CompilerParams(
            collective_id=0, has_side_effects=True, vmem_limit_bytes=40 * 1024 * 1024
        ),
    )(projections, tile_lists, band_weights, band_offsets, strip)


def from_behind(block, axis, distance):
    devices = range(lax.axis_size(axis))
    route = [((i - distance) % len(devices), i) for i in devices]
    return lax.ppermute(block, axis, route)


def ramp_block(detector_cols, first_col, block_cols):
    row_pos = lax.broadcasted_iota(jnp.float32, (detector_cols, block_cols), 0)
    col_pos = lax.broadcasted_iota(jnp.float32, (detector_cols, block_cols), 1) + first_col
    distance = col_pos - row_pos
    parity = jnp.abs(distance) % 2.0
    safe_gap = jnp.where(distance == 0.0, 1.0, distance)
    taps = jnp.where(
        distance == 0.0,
        0.25,
        jnp.where(parity == 1.0, -1.0 / (math.pi * math.pi * safe_gap * safe_gap), 0.0),
    )
    return taps.astype(jnp.bfloat16)


def ramp_filter(projection):
    view_count, row_count, detector_cols = projection.shape
    flattened = projection.reshape(view_count * row_count, detector_cols)
    block_cols = min(detector_cols, 512)
    pieces = [
        jnp.dot(
            flattened,
            ramp_block(detector_cols, first_col, block_cols),
            preferred_element_type=jnp.float32,
        )
        for first_col in range(0, detector_cols, block_cols)
    ]
    return (
        jnp.concatenate(pieces, axis=1)
        .astype(jnp.bfloat16)
        .reshape(view_count, row_count, detector_cols)
    )


def body(projections, tile_lists, band_weights, band_offsets):
    filtered = ramp_filter(projections)
    view_count, tile_rows, detector_cols = filtered.shape
    picked = tile_lists[:, 0, :]
    needed = picked.shape[1]
    tile_count = lax.axis_size(("slab", "row"))
    gathered = lax.all_gather(filtered, ("slab", "row"), axis=1, tiled=True)
    stacked = gathered.reshape(view_count, tile_count, tile_rows, detector_cols)
    chosen = jnp.take_along_axis(stacked, picked[:, :, None, None], axis=1).reshape(
        view_count, needed * tile_rows, detector_cols
    )
    band_width = band_weights.shape[3]
    y_total = band_weights.shape[1]
    z_group = band_weights.shape[2]
    cycle_size = lax.axis_size("angle")
    y_block = y_total // cycle_size
    cycle_index = lax.axis_index("angle")
    positions = jnp.arange(needed * tile_rows, dtype=jnp.int32)

    def project(y_start, y_count, z_start, z_count):
        y_first = jnp.asarray(y_start)
        zero_index = jnp.int32(0)
        z_first = jnp.int32(z_start)
        weights = lax.dynamic_slice(
            band_weights,
            (zero_index, y_first, z_first, zero_index),
            (view_count, y_count, z_count, band_width),
        )
        offsets = lax.dynamic_slice(
            band_offsets, (zero_index, y_first, z_first), (view_count, y_count, z_count)
        )
        dense_rows = jnp.zeros((view_count, y_count, z_count, needed * tile_rows), jnp.float32)
        for offset_step in range(band_width):
            matched = positions[None, None, None, :] == offsets[..., None] + offset_step
            dense_rows = dense_rows + jnp.where(
                matched, weights[..., offset_step : offset_step + 1].astype(jnp.float32), 0.0
            )
        dense_rows = dense_rows.astype(jnp.bfloat16).reshape(
            view_count, y_count * z_count, needed * tile_rows
        )
        summed = jnp.einsum("vlp,vpu->lu", dense_rows, chosen, preferred_element_type=jnp.float32)
        return summed.reshape(y_count, z_count, detector_cols)

    def forward_block(step):
        return (cycle_index - step - 1) % cycle_size * y_block

    def advance_one(step, carried):
        moved = from_behind(carried, "angle", 1)
        return moved + project(forward_block(step), y_block, 0, z_group)

    total = lax.fori_loop(
        1, cycle_size, advance_one, project(forward_block(0), y_block, 0, z_group)
    )
    return total * (math.pi / (view_count * cycle_size))


def solution(mesh):
    placed = (
        P(("groups", "angle"), ("slab", "row"), None),
        P(("groups", "angle"), ("slab", "row"), None),
        P(("groups", "angle"), None, ("slab", "row"), None),
        P(("groups", "angle"), None, ("slab", "row")),
    )
    small = (mesh.shape["angle"], mesh.shape["slab"], mesh.shape["row"]) == (4, 2, 2)
    return jax.shard_map(
        functools.partial(fused_body, mesh.shape["angle"]) if small else body,
        mesh=mesh,
        in_specs=placed,
        out_specs=P(("groups", "angle"), ("slab", "row"), None),
        check_vma=False,
    )
```

```python
import functools
import math

import jax
import jax.numpy as jnp
import ml_dtypes
import numpy as np
from jax import lax
from jax.experimental import pallas as pl
from jax.experimental.pallas import tpu as pltpu
from jax.sharding import PartitionSpec as P

MESH = pl.DeviceIdType.MESH
BLOCK = 256
WIDTHS = (512, 512, 512, 512)


def ramp_strip(detector_cols, width):
    rows = np.arange(2 * detector_cols - width)[:, None]
    gap = np.arange(width)[None, :] + (detector_cols - width) - rows
    gap32 = np.where(gap == 0, 1, gap).astype(np.float32)
    scale = np.float32(math.pi * math.pi)
    odd = np.where(gap % 2 != 0, np.float32(-1.0) / (scale * gap32 * gap32), np.float32(0.0))
    return np.where(gap == 0, np.float32(0.25), odd).astype(ml_dtypes.bfloat16)


def fused_kernel(
    angles, widths,
    x_hbm, lists_hbm, weights_hbm, offsets_hbm, strip_hbm,
    out_ref,
    x_v, lists_v, weights_v, offsets_v, strip_v,
    tables, wmat, filtered, keep, core_out, core_in, slab_out, slab_in, pair_out, pair_in, cross_out, cross_in,
    load_sem, tsend_sem, trecv_sem, csend_sem, crecv_sem, ssend_sem, srecv_sem, asend_sem, arecv_sem,
):
    views, tile_rows, cols = x_v.shape
    ys, band, zs = weights_v.shape[1:]
    lines = ys * zs
    share = lines // angles
    depth = views * tile_rows
    chunks = len(widths)
    firsts = [sum(widths[:c]) for c in range(chunks)]
    taps_wide = views * ys * band
    angle = lax.axis_index("angle")
    slab = lax.axis_index("slab")
    row = lax.axis_index("row")

    barrier = pltpu.get_barrier_semaphore()
    near_ids = [
        {"slab": 1 - slab, "row": 1 - row},
        {"slab": slab, "row": 1 - row},
        {"slab": 1 - slab, "row": row},
    ]
    half, parity = angle // 2, lax.rem(angle, 2)
    far_ids = [{"angle": 2 * half + 1 - parity}, {"angle": 2 * (1 - half) + parity}]
    for device in near_ids + far_ids:
        pl.semaphore_signal(barrier, inc=1, device_id=device, device_id_type=MESH)

    loads = [
        pltpu.make_async_copy(src, dst, load_sem.at[i])
        for i, (src, dst) in enumerate(
            [
                (lists_hbm, lists_v),
                (weights_hbm, weights_v),
                (offsets_hbm, offsets_v),
                (x_hbm, x_v),
                (strip_hbm, strip_v),
            ]
        )
    ]
    for load in loads:
        load.start()
    for load in loads[:3]:
        load.wait()

    same = lax.broadcasted_iota(jnp.int32, (zs, zs), 0) == lax.broadcasted_iota(jnp.int32, (zs, zs), 1)
    same = same.astype(jnp.float32).astype(jnp.bfloat16)

    def upright(pieces):
        flat = jnp.concatenate(pieces, axis=0).astype(jnp.bfloat16)
        return lax.dot_general(
            same, flat, (((1,), (1,)), ((), ())), preferred_element_type=jnp.float32
        )

    tables[3, :, :taps_wide] = upright(
        [weights_v[v, y].astype(jnp.float32) for v in range(views) for y in range(ys)]
    )
    spare = tables.shape[2] - taps_wide
    first_rows = upright(
        [offsets_v[v].astype(jnp.float32) for v in range(views)]
        + [jnp.zeros((spare - views * ys, zs), jnp.float32)]
    )
    lane = lax.broadcasted_iota(jnp.int32, (zs, spare), 1)
    for v in range(views):
        start = lists_v[0].astype(jnp.float32)[0:1, v : v + 1] * float(tile_rows)
        first_rows = first_rows + jnp.where((lane >= v * ys) & (lane < (v + 1) * ys), start, 0.0)
    tables[3, :, taps_wide:] = first_rows

    pl.semaphore_wait(barrier, len(near_ids) + len(far_ids))
    tcopies = [
        pltpu.make_async_remote_copy(
            src_ref=tables.at[3], dst_ref=tables.at[slot],
            send_sem=tsend_sem.at[slot], recv_sem=trecv_sem.at[slot],
            device_id=near_ids[slot], device_id_type=MESH,
        )
        for slot in range(3)
    ]
    for copy in tcopies:
        copy.start()
    for load in loads[3:]:
        load.wait()

    def build_bands():
        wide = (lines, 2 * tile_rows)
        lane = lax.broadcasted_iota(jnp.int32, wide, 1)
        second = lane >= tile_rows
        place = jnp.where(second, lane - tile_rows, lane) + (slab * 2 + row) * tile_rows
        place = place.astype(jnp.float32)

        def stretch(table, first, stride):
            return jnp.concatenate(
                [
                    jnp.broadcast_to(
                        table[:, first + y * stride : first + y * stride + 1], (zs, 2 * tile_rows)
                    )
                    for y in range(ys)
                ],
                axis=0,
            )

        for slot in range(4):
            table = tables[slot]
            for pair in range(views // 2):
                a, b = 2 * pair, 2 * pair + 1
                gap = place - jnp.where(
                    second,
                    stretch(table, taps_wide + b * ys, 1),
                    stretch(table, taps_wide + a * ys, 1),
                )
                total = jnp.zeros(wide, jnp.float32)
                for k in range(band):
                    tap = jnp.where(
                        second,
                        stretch(table, b * ys * band + k, band),
                        stretch(table, a * ys * band + k, band),
                    )
                    total = total + jnp.where(gap == float(k), tap, 0.0)
                where = pl.ds(pair * 2 * tile_rows, 2 * tile_rows)
                wmat[slot, :, where] = total.astype(jnp.bfloat16)

    def core_copy(c):
        return pltpu.make_async_remote_copy(
            src_ref=core_out[c], dst_ref=core_in[c],
            send_sem=csend_sem.at[c], recv_sem=crecv_sem.at[c],
            device_id=near_ids[1], device_id_type=MESH,
        )

    def slab_copy(c):
        return pltpu.make_async_remote_copy(
            src_ref=slab_out[c], dst_ref=slab_in[c],
            send_sem=ssend_sem.at[c], recv_sem=srecv_sem.at[c],
            device_id=near_ids[2], device_id_type=MESH,
        )

    def pair_copy(c):
        return pltpu.make_async_remote_copy(
            src_ref=pair_out[c].at[:, 1 - parity], dst_ref=pair_in[c],
            send_sem=asend_sem.at[c, 0], recv_sem=arecv_sem.at[c, 0],
            device_id=far_ids[0], device_id_type=MESH,
        )

    def cross_copy(c):
        return pltpu.make_async_remote_copy(
            src_ref=cross_out[c], dst_ref=cross_in[c],
            send_sem=asend_sem.at[c, 1], recv_sem=arecv_sem.at[c, 1],
            device_id=far_ids[1], device_id_type=MESH,
        )

    def filter_chunk(c):
        x = x_v[...].reshape(depth, cols)
        for at in range(0, widths[c], BLOCK):
            filtered[c][:, at : at + BLOCK] = jnp.dot(
                x,
                strip_v[pl.ds(cols - BLOCK - firsts[c] - at, cols), :],
                preferred_element_type=jnp.float32,
            ).astype(jnp.bfloat16)

    def project_chunk(c):
        part = jnp.dot(
            wmat[...].reshape(4 * lines, depth), filtered[c][...], preferred_element_type=jnp.float32
        )
        core_out[c][...] = part[: 2 * lines].astype(jnp.bfloat16)
        core_copy(c).start()
        keep[c][...] = part[2 * lines :]

    def core_step(c):
        core_copy(c).wait_recv()
        slab_out[c][...] = (keep[c][:lines] + core_in[c][:lines].astype(jnp.float32)).astype(jnp.bfloat16)
        slab_copy(c).start()
        keep[c][lines:] = keep[c][lines:] + core_in[c][lines:].astype(jnp.float32)

    def slab_step(c):
        slab_copy(c).wait_recv()
        total = keep[c][lines:] + slab_in[c][...].astype(jnp.float32)
        pair_out[c][...] = total.astype(jnp.bfloat16).reshape(2, 2, share, widths[c])
        pair_copy(c).start()
        keep[c][lines:] = total

    def pair_sum(c, other):
        first = pl.multiple_of(lines + (2 * other + parity) * share, share)
        return keep[c][pl.ds(first, share)] + pair_in[c][other].astype(jnp.float32)

    def pair_step(c):
        pair_copy(c).wait_recv()
        cross_out[c][...] = pair_sum(c, 1 - half).astype(jnp.bfloat16)
        cross_copy(c).start()

    def cross_step(c):
        cross_copy(c).wait_recv()
        total = pair_sum(c, half) + cross_in[c][...].astype(jnp.float32)
        out_ref[:, :, firsts[c] : firsts[c] + widths[c]] = total.reshape(share // zs, zs, widths[c])

    for c in range(chunks):
        filter_chunk(c)
    for copy in tcopies:
        copy.wait_recv()
    build_bands()
    for c in range(chunks):
        project_chunk(c)
    for c in range(chunks):
        core_step(c)
    for step in range(chunks + 1):
        if step < chunks:
            slab_step(step)
        if step >= 1:
            pair_step(step - 1)
    for c in range(chunks):
        cross_step(c)
    for copy in tcopies:
        copy.wait_send()
    for c in range(chunks):
        core_copy(c).wait_send()
        slab_copy(c).wait_send()
        pair_copy(c).wait_send()
        cross_copy(c).wait_send()


def fused_body(angles, projections, tile_lists, band_weights, band_offsets):
    views, tile_rows, cols = projections.shape
    ys, zs, band = band_weights.shape[1:]
    lines = ys * zs
    share = lines // angles
    widths = WIDTHS
    chunks = len(widths)
    strip = jnp.asarray(ramp_strip(cols, BLOCK))
    tile_lists = jnp.transpose(tile_lists, (1, 2, 0))
    band_weights = jnp.transpose(band_weights, (0, 1, 3, 2))
    table_wide = views * ys * band + -(-views * ys // 128) * 128
    bf16, f32 = jnp.bfloat16, jnp.float32
    dma = pltpu.SemaphoreType.DMA
    total = pl.pallas_call(
        functools.partial(fused_kernel, angles, widths),
        out_shape=jax.ShapeDtypeStruct((ys // angles, zs, cols), f32),
        in_specs=[pl.BlockSpec(memory_space=pl.ANY)] * 5,
        out_specs=pl.BlockSpec(memory_space=pltpu.VMEM),
        scratch_shapes=[
            pltpu.VMEM(projections.shape, bf16),
            pltpu.VMEM(tile_lists.shape, jnp.int32),
            pltpu.VMEM(band_weights.shape, bf16),
            pltpu.VMEM(band_offsets.shape, jnp.int32),
            pltpu.VMEM(strip.shape, bf16),
            pltpu.VMEM((4, zs, table_wide), f32),
            pltpu.VMEM((4, lines, views * tile_rows), bf16),
            [pltpu.VMEM((views * tile_rows, w), bf16) for w in widths],
            [pltpu.VMEM((2 * lines, w), f32) for w in widths],
            [pltpu.VMEM((2 * lines, w), bf16) for w in widths],
            [pltpu.VMEM((2 * lines, w), bf16) for w in widths],
            [pltpu.VMEM((lines, w), bf16) for w in widths],
            [pltpu.VMEM((lines, w), bf16) for w in widths],
            [pltpu.VMEM((2, 2, share, w), bf16) for w in widths],
            [pltpu.VMEM((2, share, w), bf16) for w in widths],
            [pltpu.VMEM((share, w), bf16) for w in widths],
            [pltpu.VMEM((share, w), bf16) for w in widths],
            dma((5,)),
            dma((3,)),
            dma((3,)),
            dma((chunks,)),
            dma((chunks,)),
            dma((chunks,)),
            dma((chunks,)),
            dma((chunks, 2)),
            dma((chunks, 2)),
        ],
        compiler_params=pltpu.CompilerParams(
            collective_id=0, has_side_effects=True, vmem_limit_bytes=65000 * 1024
        ),
    )(projections, tile_lists, band_weights, band_offsets, strip)
    return total * (math.pi / (views * angles))


def from_behind(block, axis, distance):
    devices = range(lax.axis_size(axis))
    route = [((i - distance) % len(devices), i) for i in devices]
    return lax.ppermute(block, axis, route)


def ramp_block(detector_cols, first_col, block_cols):
    row_pos = lax.broadcasted_iota(jnp.float32, (detector_cols, block_cols), 0)
    col_pos = lax.broadcasted_iota(jnp.float32, (detector_cols, block_cols), 1) + first_col
    distance = col_pos - row_pos
    parity = jnp.abs(distance) % 2.0
    safe_gap = jnp.where(distance == 0.0, 1.0, distance)
    taps = jnp.where(
        distance == 0.0,
        0.25,
        jnp.where(parity == 1.0, -1.0 / (math.pi * math.pi * safe_gap * safe_gap), 0.0),
    )
    return taps.astype(jnp.bfloat16)


def ramp_filter(projection):
    view_count, row_count, detector_cols = projection.shape
    flattened = projection.reshape(view_count * row_count, detector_cols)
    block_cols = min(detector_cols, 512)
    pieces = [
        jnp.dot(
            flattened,
            ramp_block(detector_cols, first_col, block_cols),
            preferred_element_type=jnp.float32,
        )
        for first_col in range(0, detector_cols, block_cols)
    ]
    return (
        jnp.concatenate(pieces, axis=1)
        .astype(jnp.bfloat16)
        .reshape(view_count, row_count, detector_cols)
    )


def body(projections, tile_lists, band_weights, band_offsets):
    filtered = ramp_filter(projections)
    view_count, tile_rows, detector_cols = filtered.shape
    picked = tile_lists[:, 0, :]
    needed = picked.shape[1]
    tile_count = lax.axis_size(("slab", "row"))
    gathered = lax.all_gather(filtered, ("slab", "row"), axis=1, tiled=True)
    stacked = gathered.reshape(view_count, tile_count, tile_rows, detector_cols)
    chosen = jnp.take_along_axis(stacked, picked[:, :, None, None], axis=1).reshape(
        view_count, needed * tile_rows, detector_cols
    )
    band_width = band_weights.shape[3]
    y_total = band_weights.shape[1]
    z_group = band_weights.shape[2]
    cycle_size = lax.axis_size("angle")
    y_block = y_total // cycle_size
    cycle_index = lax.axis_index("angle")
    positions = jnp.arange(needed * tile_rows, dtype=jnp.int32)

    def project(y_start, y_count, z_start, z_count):
        y_first = jnp.asarray(y_start)
        zero_index = jnp.int32(0)
        z_first = jnp.int32(z_start)
        weights = lax.dynamic_slice(
            band_weights,
            (zero_index, y_first, z_first, zero_index),
            (view_count, y_count, z_count, band_width),
        )
        offsets = lax.dynamic_slice(
            band_offsets, (zero_index, y_first, z_first), (view_count, y_count, z_count)
        )
        dense_rows = jnp.zeros((view_count, y_count, z_count, needed * tile_rows), jnp.float32)
        for offset_step in range(band_width):
            matched = positions[None, None, None, :] == offsets[..., None] + offset_step
            dense_rows = dense_rows + jnp.where(
                matched, weights[..., offset_step : offset_step + 1].astype(jnp.float32), 0.0
            )
        dense_rows = dense_rows.astype(jnp.bfloat16).reshape(
            view_count, y_count * z_count, needed * tile_rows
        )
        summed = jnp.einsum("vlp,vpu->lu", dense_rows, chosen, preferred_element_type=jnp.float32)
        return summed.reshape(y_count, z_count, detector_cols)

    def forward_block(step):
        return (cycle_index - step - 1) % cycle_size * y_block

    def advance_one(step, carried):
        moved = from_behind(carried, "angle", 1)
        return moved + project(forward_block(step), y_block, 0, z_group)

    total = lax.fori_loop(
        1, cycle_size, advance_one, project(forward_block(0), y_block, 0, z_group)
    )
    return total * (math.pi / (view_count * cycle_size))


def solution(mesh):
    placed = (
        P(("groups", "angle"), ("slab", "row"), None),
        P(("groups", "angle"), ("slab", "row"), None),
        P(("groups", "angle"), None, ("slab", "row"), None),
        P(("groups", "angle"), None, ("slab", "row")),
    )
    small = (mesh.shape["angle"], mesh.shape["slab"], mesh.shape["row"]) == (4, 2, 2)
    return jax.shard_map(
        functools.partial(fused_body, mesh.shape["angle"]) if small else body,
        mesh=mesh,
        in_specs=placed,
        out_specs=P(("groups", "angle"), ("slab", "row"), None),
        check_vma=False,
    )
```

```python
import functools
import math

import jax
import jax.numpy as jnp
import ml_dtypes
import numpy as np
from jax import lax
from jax.experimental import pallas as pl
from jax.experimental.pallas import tpu as pltpu
from jax.sharding import PartitionSpec as P

MESH = pl.DeviceIdType.MESH
BLOCK = 256
WIDTHS = (512, 512, 512, 512)


def ramp_strip(detector_cols, width):
    rows = np.arange(2 * detector_cols - width)[:, None]
    gap = np.arange(width)[None, :] + (detector_cols - width) - rows
    gap32 = np.where(gap == 0, 1, gap).astype(np.float32)
    scale = np.float32(math.pi * math.pi)
    odd = np.where(gap % 2 != 0, np.float32(-1.0) / (scale * gap32 * gap32), np.float32(0.0))
    return np.where(gap == 0, np.float32(0.25), odd).astype(ml_dtypes.bfloat16)


def fused_kernel(
    angles, widths,
    x_hbm, lists_hbm, weights_hbm, offsets_hbm, strip_hbm,
    out_ref,
    x_v, lists_v, weights_v, offsets_v, strip_v,
    tables, wmat, filtered, keep, core_out, core_in, slab_out, slab_in, angle_out, angle_in,
    load_sem, tsend_sem, trecv_sem, csend_sem, crecv_sem, ssend_sem, srecv_sem, asend_sem, arecv_sem,
):
    views, tile_rows, cols = x_v.shape
    ys, band, zs = weights_v.shape[1:]
    lines = ys * zs
    share = lines // angles
    depth = views * tile_rows
    chunks = len(widths)
    firsts = [sum(widths[:c]) for c in range(chunks)]
    taps_wide = views * ys * band
    angle = lax.axis_index("angle")
    slab = lax.axis_index("slab")
    row = lax.axis_index("row")

    barrier = pltpu.get_barrier_semaphore()
    near_ids = [
        {"slab": 1 - slab, "row": 1 - row},
        {"slab": slab, "row": 1 - row},
        {"slab": 1 - slab, "row": row},
    ]
    far_ids = [{"angle": lax.rem(angle + j, angles)} for j in range(1, angles)]
    for device in near_ids + far_ids:
        pl.semaphore_signal(barrier, inc=1, device_id=device, device_id_type=MESH)

    loads = [
        pltpu.make_async_copy(src, dst, load_sem.at[i])
        for i, (src, dst) in enumerate(
            [
                (lists_hbm, lists_v),
                (weights_hbm, weights_v),
                (offsets_hbm, offsets_v),
                (x_hbm, x_v),
                (strip_hbm, strip_v),
            ]
        )
    ]
    for load in loads:
        load.start()
    for load in loads[:3]:
        load.wait()

    same = lax.broadcasted_iota(jnp.int32, (zs, zs), 0) == lax.broadcasted_iota(jnp.int32, (zs, zs), 1)
    same = same.astype(jnp.float32).astype(jnp.bfloat16)

    def upright(pieces):
        flat = jnp.concatenate(pieces, axis=0).astype(jnp.bfloat16)
        return lax.dot_general(
            same, flat, (((1,), (1,)), ((), ())), preferred_element_type=jnp.float32
        )

    tables[3, :, :taps_wide] = upright(
        [weights_v[v, y].astype(jnp.float32) for v in range(views) for y in range(ys)]
    )
    spare = tables.shape[2] - taps_wide
    first_rows = upright(
        [offsets_v[v].astype(jnp.float32) for v in range(views)]
        + [jnp.zeros((spare - views * ys, zs), jnp.float32)]
    )
    lane = lax.broadcasted_iota(jnp.int32, (zs, spare), 1)
    for v in range(views):
        start = lists_v[0].astype(jnp.float32)[0:1, v : v + 1] * float(tile_rows)
        first_rows = first_rows + jnp.where((lane >= v * ys) & (lane < (v + 1) * ys), start, 0.0)
    tables[3, :, taps_wide:] = first_rows

    pl.semaphore_wait(barrier, len(near_ids) + len(far_ids))
    tcopies = [
        pltpu.make_async_remote_copy(
            src_ref=tables.at[3], dst_ref=tables.at[slot],
            send_sem=tsend_sem.at[slot], recv_sem=trecv_sem.at[slot],
            device_id=near_ids[slot], device_id_type=MESH,
        )
        for slot in range(3)
    ]
    for copy in tcopies:
        copy.start()
    for load in loads[3:]:
        load.wait()

    def build_bands():
        wide = (lines, 2 * tile_rows)
        lane = lax.broadcasted_iota(jnp.int32, wide, 1)
        second = lane >= tile_rows
        place = jnp.where(second, lane - tile_rows, lane) + (slab * 2 + row) * tile_rows
        place = place.astype(jnp.float32)

        def stretch(table, first, stride):
            return jnp.concatenate(
                [
                    jnp.broadcast_to(
                        table[:, first + y * stride : first + y * stride + 1], (zs, 2 * tile_rows)
                    )
                    for y in range(ys)
                ],
                axis=0,
            )

        for slot in range(4):
            table = tables[slot]
            for pair in range(views // 2):
                a, b = 2 * pair, 2 * pair + 1
                gap = place - jnp.where(
                    second,
                    stretch(table, taps_wide + b * ys, 1),
                    stretch(table, taps_wide + a * ys, 1),
                )
                total = jnp.zeros(wide, jnp.float32)
                for k in range(band):
                    tap = jnp.where(
                        second,
                        stretch(table, b * ys * band + k, band),
                        stretch(table, a * ys * band + k, band),
                    )
                    total = total + jnp.where(gap == float(k), tap, 0.0)
                where = pl.ds(pair * 2 * tile_rows, 2 * tile_rows)
                wmat[slot, :, where] = total.astype(jnp.bfloat16)

    def core_copy(c):
        return pltpu.make_async_remote_copy(
            src_ref=core_out[c], dst_ref=core_in[c],
            send_sem=csend_sem.at[c], recv_sem=crecv_sem.at[c],
            device_id=near_ids[1], device_id_type=MESH,
        )

    def slab_copy(c):
        return pltpu.make_async_remote_copy(
            src_ref=slab_out[c], dst_ref=slab_in[c],
            send_sem=ssend_sem.at[c], recv_sem=srecv_sem.at[c],
            device_id=near_ids[2], device_id_type=MESH,
        )

    def angle_copy(c, j):
        there = pl.multiple_of(lax.rem(angle + j, angles) * share, share)
        return pltpu.make_async_remote_copy(
            src_ref=angle_out[c].at[pl.ds(there, share)], dst_ref=angle_in[c].at[j - 1],
            send_sem=asend_sem.at[c, j - 1], recv_sem=arecv_sem.at[c, j - 1],
            device_id=far_ids[j - 1], device_id_type=MESH,
        )

    def filter_chunk(c):
        x = x_v[...].reshape(depth, cols)
        for at in range(0, widths[c], BLOCK):
            filtered[c][:, at : at + BLOCK] = jnp.dot(
                x,
                strip_v[pl.ds(cols - BLOCK - firsts[c] - at, cols), :],
                preferred_element_type=jnp.float32,
            ).astype(jnp.bfloat16)

    def project_chunk(c):
        part = jnp.dot(
            wmat[...].reshape(4 * lines, depth), filtered[c][...], preferred_element_type=jnp.float32
        )
        core_out[c][...] = part[: 2 * lines].astype(jnp.bfloat16)
        core_copy(c).start()
        keep[c][...] = part[2 * lines :]

    def core_step(c):
        core_copy(c).wait_recv()
        slab_out[c][...] = (keep[c][:lines] + core_in[c][:lines].astype(jnp.float32)).astype(jnp.bfloat16)
        slab_copy(c).start()
        keep[c][lines:] = keep[c][lines:] + core_in[c][lines:].astype(jnp.float32)

    def slab_step(c):
        slab_copy(c).wait_recv()
        total = keep[c][lines:] + slab_in[c][...].astype(jnp.float32)
        angle_out[c][...] = total.astype(jnp.bfloat16)
        for j in range(1, angles):
            angle_copy(c, j).start()
        keep[c][lines:] = total

    def angle_step(c):
        here = pl.multiple_of(angle * share, share)
        total = keep[c][pl.ds(lines + here, share)]
        for j in range(1, angles):
            angle_copy(c, j).wait_recv()
            total = total + angle_in[c][j - 1].astype(jnp.float32)
        out_ref[:, :, firsts[c] : firsts[c] + widths[c]] = total.reshape(share // zs, zs, widths[c])

    for c in range(chunks):
        filter_chunk(c)
    for copy in tcopies:
        copy.wait_recv()
    build_bands()
    for c in range(chunks):
        project_chunk(c)
    for c in range(chunks):
        core_step(c)
    for c in range(chunks):
        slab_step(c)
    for c in range(chunks):
        angle_step(c)
    for copy in tcopies:
        copy.wait_send()
    for c in range(chunks):
        core_copy(c).wait_send()
        slab_copy(c).wait_send()
        for j in range(1, angles):
            angle_copy(c, j).wait_send()


def fused_body(angles, projections, tile_lists, band_weights, band_offsets):
    views, tile_rows, cols = projections.shape
    ys, zs, band = band_weights.shape[1:]
    lines = ys * zs
    share = lines // angles
    widths = WIDTHS
    chunks = len(widths)
    strip = jnp.asarray(ramp_strip(cols, BLOCK))
    tile_lists = jnp.transpose(tile_lists, (1, 2, 0))
    band_weights = jnp.transpose(band_weights, (0, 1, 3, 2))
    table_wide = views * ys * band + -(-views * ys // 128) * 128
    bf16, f32 = jnp.bfloat16, jnp.float32
    dma = pltpu.SemaphoreType.DMA
    total = pl.pallas_call(
        functools.partial(fused_kernel, angles, widths),
        out_shape=jax.ShapeDtypeStruct((ys // angles, zs, cols), f32),
        in_specs=[pl.BlockSpec(memory_space=pl.ANY)] * 5,
        out_specs=pl.BlockSpec(memory_space=pltpu.VMEM),
        scratch_shapes=[
            pltpu.VMEM(projections.shape, bf16),
            pltpu.VMEM(tile_lists.shape, jnp.int32),
            pltpu.VMEM(band_weights.shape, bf16),
            pltpu.VMEM(band_offsets.shape, jnp.int32),
            pltpu.VMEM(strip.shape, bf16),
            pltpu.VMEM((4, zs, table_wide), f32),
            pltpu.VMEM((4, lines, views * tile_rows), bf16),
            [pltpu.VMEM((views * tile_rows, w), bf16) for w in widths],
            [pltpu.VMEM((2 * lines, w), f32) for w in widths],
            [pltpu.VMEM((2 * lines, w), bf16) for w in widths],
            [pltpu.VMEM((2 * lines, w), bf16) for w in widths],
            [pltpu.VMEM((lines, w), bf16) for w in widths],
            [pltpu.VMEM((lines, w), bf16) for w in widths],
            [pltpu.VMEM((lines, w), bf16) for w in widths],
            [pltpu.VMEM((angles - 1, share, w), bf16) for w in widths],
            dma((5,)),
            dma((3,)),
            dma((3,)),
            dma((chunks,)),
            dma((chunks,)),
            dma((chunks,)),
            dma((chunks,)),
            dma((chunks, angles - 1)),
            dma((chunks, angles - 1)),
        ],
        compiler_params=pltpu.CompilerParams(
            collective_id=0, has_side_effects=True, vmem_limit_bytes=65000 * 1024
        ),
    )(projections, tile_lists, band_weights, band_offsets, strip)
    return total * (math.pi / (views * angles))


def from_behind(block, axis, distance):
    devices = range(lax.axis_size(axis))
    route = [((i - distance) % len(devices), i) for i in devices]
    return lax.ppermute(block, axis, route)


def ramp_block(detector_cols, first_col, block_cols):
    row_pos = lax.broadcasted_iota(jnp.float32, (detector_cols, block_cols), 0)
    col_pos = lax.broadcasted_iota(jnp.float32, (detector_cols, block_cols), 1) + first_col
    distance = col_pos - row_pos
    parity = jnp.abs(distance) % 2.0
    safe_gap = jnp.where(distance == 0.0, 1.0, distance)
    taps = jnp.where(
        distance == 0.0,
        0.25,
        jnp.where(parity == 1.0, -1.0 / (math.pi * math.pi * safe_gap * safe_gap), 0.0),
    )
    return taps.astype(jnp.bfloat16)


def ramp_filter(projection):
    view_count, row_count, detector_cols = projection.shape
    flattened = projection.reshape(view_count * row_count, detector_cols)
    block_cols = min(detector_cols, 512)
    pieces = [
        jnp.dot(
            flattened,
            ramp_block(detector_cols, first_col, block_cols),
            preferred_element_type=jnp.float32,
        )
        for first_col in range(0, detector_cols, block_cols)
    ]
    return (
        jnp.concatenate(pieces, axis=1)
        .astype(jnp.bfloat16)
        .reshape(view_count, row_count, detector_cols)
    )


def body(projections, tile_lists, band_weights, band_offsets):
    filtered = ramp_filter(projections)
    view_count, tile_rows, detector_cols = filtered.shape
    picked = tile_lists[:, 0, :]
    needed = picked.shape[1]
    tile_count = lax.axis_size(("slab", "row"))
    gathered = lax.all_gather(filtered, ("slab", "row"), axis=1, tiled=True)
    stacked = gathered.reshape(view_count, tile_count, tile_rows, detector_cols)
    chosen = jnp.take_along_axis(stacked, picked[:, :, None, None], axis=1).reshape(
        view_count, needed * tile_rows, detector_cols
    )
    band_width = band_weights.shape[3]
    y_total = band_weights.shape[1]
    z_group = band_weights.shape[2]
    cycle_size = lax.axis_size("angle")
    y_block = y_total // cycle_size
    cycle_index = lax.axis_index("angle")
    positions = jnp.arange(needed * tile_rows, dtype=jnp.int32)

    def project(y_start, y_count, z_start, z_count):
        y_first = jnp.asarray(y_start)
        zero_index = jnp.int32(0)
        z_first = jnp.int32(z_start)
        weights = lax.dynamic_slice(
            band_weights,
            (zero_index, y_first, z_first, zero_index),
            (view_count, y_count, z_count, band_width),
        )
        offsets = lax.dynamic_slice(
            band_offsets, (zero_index, y_first, z_first), (view_count, y_count, z_count)
        )
        dense_rows = jnp.zeros((view_count, y_count, z_count, needed * tile_rows), jnp.float32)
        for offset_step in range(band_width):
            matched = positions[None, None, None, :] == offsets[..., None] + offset_step
            dense_rows = dense_rows + jnp.where(
                matched, weights[..., offset_step : offset_step + 1].astype(jnp.float32), 0.0
            )
        dense_rows = dense_rows.astype(jnp.bfloat16).reshape(
            view_count, y_count * z_count, needed * tile_rows
        )
        summed = jnp.einsum("vlp,vpu->lu", dense_rows, chosen, preferred_element_type=jnp.float32)
        return summed.reshape(y_count, z_count, detector_cols)

    def forward_block(step):
        return (cycle_index - step - 1) % cycle_size * y_block

    def advance_one(step, carried):
        moved = from_behind(carried, "angle", 1)
        return moved + project(forward_block(step), y_block, 0, z_group)

    total = lax.fori_loop(
        1, cycle_size, advance_one, project(forward_block(0), y_block, 0, z_group)
    )
    return total * (math.pi / (view_count * cycle_size))


def solution(mesh):
    placed = (
        P(("groups", "angle"), ("slab", "row"), None),
        P(("groups", "angle"), ("slab", "row"), None),
        P(("groups", "angle"), None, ("slab", "row"), None),
        P(("groups", "angle"), None, ("slab", "row")),
    )
    small = (mesh.shape["angle"], mesh.shape["slab"], mesh.shape["row"]) == (4, 2, 2)
    return jax.shard_map(
        functools.partial(fused_body, mesh.shape["angle"]) if small else body,
        mesh=mesh,
        in_specs=placed,
        out_specs=P(("groups", "angle"), ("slab", "row"), None),
        check_vma=False,
    )
```

```python
import functools
import math

import jax
import jax.numpy as jnp
import ml_dtypes
import numpy as np
from jax import lax
from jax.experimental import pallas as pl
from jax.experimental.pallas import tpu as pltpu
from jax.sharding import PartitionSpec as P

MESH = pl.DeviceIdType.MESH
BLOCK = 256
WIDTHS = (256, 512, 512, 512, 256)


def ramp_strip(detector_cols, width):
    rows = np.arange(2 * detector_cols - width)[:, None]
    gap = np.arange(width)[None, :] + (detector_cols - width) - rows
    gap32 = np.where(gap == 0, 1, gap).astype(np.float32)
    scale = np.float32(math.pi * math.pi)
    odd = np.where(gap % 2 != 0, np.float32(-1.0) / (scale * gap32 * gap32), np.float32(0.0))
    return np.where(gap == 0, np.float32(0.25), odd).astype(ml_dtypes.bfloat16)


def fused_kernel(
    angles, widths,
    x_hbm, lists_hbm, weights_hbm, offsets_hbm, strip_hbm,
    out_ref,
    x_v, lists_v, weights_v, offsets_v, strip_v,
    tables, wmat, filtered, keep, core_out, core_in, slab_out, slab_in, angle_out, angle_in,
    load_sem, tsend_sem, trecv_sem, csend_sem, crecv_sem, ssend_sem, srecv_sem, asend_sem, arecv_sem,
):
    views, tile_rows, cols = x_v.shape
    ys, band, zs = weights_v.shape[1:]
    lines = ys * zs
    share = lines // angles
    depth = views * tile_rows
    chunks = len(widths)
    firsts = [sum(widths[:c]) for c in range(chunks)]
    taps_wide = views * ys * band
    angle = lax.axis_index("angle")
    slab = lax.axis_index("slab")
    row = lax.axis_index("row")

    barrier = pltpu.get_barrier_semaphore()
    near_ids = [
        {"slab": 1 - slab, "row": 1 - row},
        {"slab": slab, "row": 1 - row},
        {"slab": 1 - slab, "row": row},
    ]
    far_ids = [{"angle": lax.rem(angle + j, angles)} for j in range(1, angles)]
    for device in near_ids + far_ids:
        pl.semaphore_signal(barrier, inc=1, device_id=device, device_id_type=MESH)

    loads = [
        pltpu.make_async_copy(src, dst, load_sem.at[i])
        for i, (src, dst) in enumerate(
            [
                (lists_hbm, lists_v),
                (weights_hbm, weights_v),
                (offsets_hbm, offsets_v),
                (x_hbm, x_v),
                (strip_hbm, strip_v),
            ]
        )
    ]
    for load in loads:
        load.start()
    for load in loads[:3]:
        load.wait()

    same = lax.broadcasted_iota(jnp.int32, (zs, zs), 0) == lax.broadcasted_iota(jnp.int32, (zs, zs), 1)
    same = same.astype(jnp.float32).astype(jnp.bfloat16)

    def upright(pieces):
        flat = jnp.concatenate(pieces, axis=0).astype(jnp.bfloat16)
        return lax.dot_general(
            same, flat, (((1,), (1,)), ((), ())), preferred_element_type=jnp.float32
        )

    tables[3, :, :taps_wide] = upright(
        [weights_v[v, y].astype(jnp.float32) for v in range(views) for y in range(ys)]
    )
    spare = tables.shape[2] - taps_wide
    first_rows = upright(
        [offsets_v[v].astype(jnp.float32) for v in range(views)]
        + [jnp.zeros((spare - views * ys, zs), jnp.float32)]
    )
    lane = lax.broadcasted_iota(jnp.int32, (zs, spare), 1)
    for v in range(views):
        start = lists_v[0].astype(jnp.float32)[0:1, v : v + 1] * float(tile_rows)
        first_rows = first_rows + jnp.where((lane >= v * ys) & (lane < (v + 1) * ys), start, 0.0)
    tables[3, :, taps_wide:] = first_rows

    pl.semaphore_wait(barrier, len(near_ids) + len(far_ids))
    tcopies = [
        pltpu.make_async_remote_copy(
            src_ref=tables.at[3], dst_ref=tables.at[slot],
            send_sem=tsend_sem.at[slot], recv_sem=trecv_sem.at[slot],
            device_id=near_ids[slot], device_id_type=MESH,
        )
        for slot in range(3)
    ]
    for copy in tcopies:
        copy.start()
    for load in loads[3:]:
        load.wait()

    def build_bands():
        wide = (lines, 2 * tile_rows)
        lane = lax.broadcasted_iota(jnp.int32, wide, 1)
        second = lane >= tile_rows
        place = jnp.where(second, lane - tile_rows, lane) + (slab * 2 + row) * tile_rows
        place = place.astype(jnp.float32)

        def stretch(table, first, stride):
            return jnp.concatenate(
                [
                    jnp.broadcast_to(
                        table[:, first + y * stride : first + y * stride + 1], (zs, 2 * tile_rows)
                    )
                    for y in range(ys)
                ],
                axis=0,
            )

        for slot in range(4):
            table = tables[slot]
            for pair in range(views // 2):
                a, b = 2 * pair, 2 * pair + 1
                gap = place - jnp.where(
                    second,
                    stretch(table, taps_wide + b * ys, 1),
                    stretch(table, taps_wide + a * ys, 1),
                )
                total = jnp.zeros(wide, jnp.float32)
                for k in range(band):
                    tap = jnp.where(
                        second,
                        stretch(table, b * ys * band + k, band),
                        stretch(table, a * ys * band + k, band),
                    )
                    total = total + jnp.where(gap == float(k), tap, 0.0)
                where = pl.ds(pair * 2 * tile_rows, 2 * tile_rows)
                wmat[slot, :, where] = total.astype(jnp.bfloat16)

    def core_copy(c):
        return pltpu.make_async_remote_copy(
            src_ref=core_out[c], dst_ref=core_in[c],
            send_sem=csend_sem.at[c], recv_sem=crecv_sem.at[c],
            device_id=near_ids[1], device_id_type=MESH,
        )

    def slab_copy(c):
        return pltpu.make_async_remote_copy(
            src_ref=slab_out[c], dst_ref=slab_in[c],
            send_sem=ssend_sem.at[c], recv_sem=srecv_sem.at[c],
            device_id=near_ids[2], device_id_type=MESH,
        )

    def angle_copy(c, j):
        there = pl.multiple_of(lax.rem(angle + j, angles) * share, share)
        return pltpu.make_async_remote_copy(
            src_ref=angle_out[c].at[pl.ds(there, share)], dst_ref=angle_in[c].at[j - 1],
            send_sem=asend_sem.at[c, j - 1], recv_sem=arecv_sem.at[c, j - 1],
            device_id=far_ids[j - 1], device_id_type=MESH,
        )

    def filter_chunk(c):
        x = x_v[...].reshape(depth, cols)
        for at in range(0, widths[c], BLOCK):
            filtered[c][:, at : at + BLOCK] = jnp.dot(
                x,
                strip_v[pl.ds(cols - BLOCK - firsts[c] - at, cols), :],
                preferred_element_type=jnp.float32,
            ).astype(jnp.bfloat16)

    def project_chunk(c):
        part = jnp.dot(
            wmat[...].reshape(4 * lines, depth), filtered[c][...], preferred_element_type=jnp.float32
        )
        core_out[c][...] = part[: 2 * lines].astype(jnp.bfloat16)
        core_copy(c).start()
        keep[c][...] = part[2 * lines :]

    def core_step(c):
        core_copy(c).wait_recv()
        slab_out[c][...] = (keep[c][:lines] + core_in[c][:lines].astype(jnp.float32)).astype(jnp.bfloat16)
        slab_copy(c).start()
        keep[c][lines:] = keep[c][lines:] + core_in[c][lines:].astype(jnp.float32)

    def slab_step(c):
        slab_copy(c).wait_recv()
        total = keep[c][lines:] + slab_in[c][...].astype(jnp.float32)
        angle_out[c][...] = total.astype(jnp.bfloat16)
        for j in range(1, angles):
            angle_copy(c, j).start()
        keep[c][lines:] = total

    def angle_step(c):
        here = pl.multiple_of(angle * share, share)
        total = keep[c][pl.ds(lines + here, share)]
        for j in range(1, angles):
            angle_copy(c, j).wait_recv()
            total = total + angle_in[c][j - 1].astype(jnp.float32)
        out_ref[:, :, firsts[c] : firsts[c] + widths[c]] = total.reshape(share // zs, zs, widths[c])

    for c in range(chunks):
        filter_chunk(c)
    for copy in tcopies:
        copy.wait_recv()
    build_bands()
    for step in range(chunks + 2):
        if step < chunks:
            project_chunk(step)
        if step >= 2:
            core_step(step - 2)
    for c in range(chunks):
        slab_step(c)
    for c in range(chunks):
        angle_step(c)
    for copy in tcopies:
        copy.wait_send()
    for c in range(chunks):
        core_copy(c).wait_send()
        slab_copy(c).wait_send()
        for j in range(1, angles):
            angle_copy(c, j).wait_send()


def fused_body(angles, projections, tile_lists, band_weights, band_offsets):
    views, tile_rows, cols = projections.shape
    ys, zs, band = band_weights.shape[1:]
    lines = ys * zs
    share = lines // angles
    widths = WIDTHS
    chunks = len(widths)
    strip = jnp.asarray(ramp_strip(cols, BLOCK))
    tile_lists = jnp.transpose(tile_lists, (1, 2, 0))
    band_weights = jnp.transpose(band_weights, (0, 1, 3, 2))
    table_wide = views * ys * band + -(-views * ys // 128) * 128
    bf16, f32 = jnp.bfloat16, jnp.float32
    dma = pltpu.SemaphoreType.DMA
    total = pl.pallas_call(
        functools.partial(fused_kernel, angles, widths),
        out_shape=jax.ShapeDtypeStruct((ys // angles, zs, cols), f32),
        in_specs=[pl.BlockSpec(memory_space=pl.ANY)] * 5,
        out_specs=pl.BlockSpec(memory_space=pltpu.VMEM),
        scratch_shapes=[
            pltpu.VMEM(projections.shape, bf16),
            pltpu.VMEM(tile_lists.shape, jnp.int32),
            pltpu.VMEM(band_weights.shape, bf16),
            pltpu.VMEM(band_offsets.shape, jnp.int32),
            pltpu.VMEM(strip.shape, bf16),
            pltpu.VMEM((4, zs, table_wide), f32),
            pltpu.VMEM((4, lines, views * tile_rows), bf16),
            [pltpu.VMEM((views * tile_rows, w), bf16) for w in widths],
            [pltpu.VMEM((2 * lines, w), f32) for w in widths],
            [pltpu.VMEM((2 * lines, w), bf16) for w in widths],
            [pltpu.VMEM((2 * lines, w), bf16) for w in widths],
            [pltpu.VMEM((lines, w), bf16) for w in widths],
            [pltpu.VMEM((lines, w), bf16) for w in widths],
            [pltpu.VMEM((lines, w), bf16) for w in widths],
            [pltpu.VMEM((angles - 1, share, w), bf16) for w in widths],
            dma((5,)),
            dma((3,)),
            dma((3,)),
            dma((chunks,)),
            dma((chunks,)),
            dma((chunks,)),
            dma((chunks,)),
            dma((chunks, angles - 1)),
            dma((chunks, angles - 1)),
        ],
        compiler_params=pltpu.CompilerParams(
            collective_id=0, has_side_effects=True, vmem_limit_bytes=65000 * 1024
        ),
    )(projections, tile_lists, band_weights, band_offsets, strip)
    return total * (math.pi / (views * angles))


def from_behind(block, axis, distance):
    devices = range(lax.axis_size(axis))
    route = [((i - distance) % len(devices), i) for i in devices]
    return lax.ppermute(block, axis, route)


def ramp_block(detector_cols, first_col, block_cols):
    row_pos = lax.broadcasted_iota(jnp.float32, (detector_cols, block_cols), 0)
    col_pos = lax.broadcasted_iota(jnp.float32, (detector_cols, block_cols), 1) + first_col
    distance = col_pos - row_pos
    parity = jnp.abs(distance) % 2.0
    safe_gap = jnp.where(distance == 0.0, 1.0, distance)
    taps = jnp.where(
        distance == 0.0,
        0.25,
        jnp.where(parity == 1.0, -1.0 / (math.pi * math.pi * safe_gap * safe_gap), 0.0),
    )
    return taps.astype(jnp.bfloat16)


def ramp_filter(projection):
    view_count, row_count, detector_cols = projection.shape
    flattened = projection.reshape(view_count * row_count, detector_cols)
    block_cols = min(detector_cols, 512)
    pieces = [
        jnp.dot(
            flattened,
            ramp_block(detector_cols, first_col, block_cols),
            preferred_element_type=jnp.float32,
        )
        for first_col in range(0, detector_cols, block_cols)
    ]
    return (
        jnp.concatenate(pieces, axis=1)
        .astype(jnp.bfloat16)
        .reshape(view_count, row_count, detector_cols)
    )


def body(projections, tile_lists, band_weights, band_offsets):
    filtered = ramp_filter(projections)
    view_count, tile_rows, detector_cols = filtered.shape
    picked = tile_lists[:, 0, :]
    needed = picked.shape[1]
    tile_count = lax.axis_size(("slab", "row"))
    gathered = lax.all_gather(filtered, ("slab", "row"), axis=1, tiled=True)
    stacked = gathered.reshape(view_count, tile_count, tile_rows, detector_cols)
    chosen = jnp.take_along_axis(stacked, picked[:, :, None, None], axis=1).reshape(
        view_count, needed * tile_rows, detector_cols
    )
    band_width = band_weights.shape[3]
    y_total = band_weights.shape[1]
    z_group = band_weights.shape[2]
    cycle_size = lax.axis_size("angle")
    y_block = y_total // cycle_size
    cycle_index = lax.axis_index("angle")
    positions = jnp.arange(needed * tile_rows, dtype=jnp.int32)

    def project(y_start, y_count, z_start, z_count):
        y_first = jnp.asarray(y_start)
        zero_index = jnp.int32(0)
        z_first = jnp.int32(z_start)
        weights = lax.dynamic_slice(
            band_weights,
            (zero_index, y_first, z_first, zero_index),
            (view_count, y_count, z_count, band_width),
        )
        offsets = lax.dynamic_slice(
            band_offsets, (zero_index, y_first, z_first), (view_count, y_count, z_count)
        )
        dense_rows = jnp.zeros((view_count, y_count, z_count, needed * tile_rows), jnp.float32)
        for offset_step in range(band_width):
            matched = positions[None, None, None, :] == offsets[..., None] + offset_step
            dense_rows = dense_rows + jnp.where(
                matched, weights[..., offset_step : offset_step + 1].astype(jnp.float32), 0.0
            )
        dense_rows = dense_rows.astype(jnp.bfloat16).reshape(
            view_count, y_count * z_count, needed * tile_rows
        )
        summed = jnp.einsum("vlp,vpu->lu", dense_rows, chosen, preferred_element_type=jnp.float32)
        return summed.reshape(y_count, z_count, detector_cols)

    def forward_block(step):
        return (cycle_index - step - 1) % cycle_size * y_block

    def advance_one(step, carried):
        moved = from_behind(carried, "angle", 1)
        return moved + project(forward_block(step), y_block, 0, z_group)

    total = lax.fori_loop(
        1, cycle_size, advance_one, project(forward_block(0), y_block, 0, z_group)
    )
    return total * (math.pi / (view_count * cycle_size))


def solution(mesh):
    placed = (
        P(("groups", "angle"), ("slab", "row"), None),
        P(("groups", "angle"), ("slab", "row"), None),
        P(("groups", "angle"), None, ("slab", "row"), None),
        P(("groups", "angle"), None, ("slab", "row")),
    )
    small = (mesh.shape["angle"], mesh.shape["slab"], mesh.shape["row"]) == (4, 2, 2)
    return jax.shard_map(
        functools.partial(fused_body, mesh.shape["angle"]) if small else body,
        mesh=mesh,
        in_specs=placed,
        out_specs=P(("groups", "angle"), ("slab", "row"), None),
        check_vma=False,
    )
```
